256 devices in a mesh: group: 16 (over x, z_hi), tensor: 16 (over z_lo, y, core).
Axes of the slice: x: 4, y: 4, z: 8 (z_hi: 4, z_lo: 2; z = z_hi * 2 + z_lo), core: 2. Of those that a mesh axis runs over, the one named last changes fastest.
Arguments:
- tokens: bfloat16 [12288, 8192], P('group', 'tensor'), may hold values from -6 to 6
- base_values: bfloat16 [8192, 8192], P('tensor'), may hold values from -0.09375 to 0.09375
- base_scales: float32 [64, 64], P('tensor'), may hold values from 0.3 to 3
- shrink_factors: bfloat16 [32, 8192, 64], P('group', 'tensor'), may hold values from -0.0625 to 0.0625
- expand_factors: bfloat16 [32, 64, 8192], P('group', None, 'tensor'), may hold values from -0.75 to 0.75
- adapter_slot: int32 [32], replicated, may hold values from 0 to 31, each once
- tile_adapter: int32 [192], P('group'), may hold values from 0 to 31, as said below
- tile_count: int32 [192], P('group'), may hold values from 1 to 64, as said below
Outputs:
- mixed: bfloat16 [12288, 8192], P('group', 'tensor')
The draws below stay inside these ranges and needn't reach their ends.
Inputs may be any that keep to these rules, and one draw needn't show every extreme that they name: `tile_adapter`: every adapter is named by at least one segment. `tile_count`: the first segment of each group's rows is full.
All inputs are finite; a program needn't handle non-finite values.
Results may differ from the reference program's by a relative error of at most 0.023.
Values may be sent and summed in bfloat16 or wider, within the bound.
No kernel may reach another device: no remote copies, remote signals or barrier semaphores. Data moves between devices by JAX's collectives and lax.ppermute only.
A program may use at most 128 MiB of HBM per device.

```python
import math
import jax
import jax.numpy as jnp
from jax import lax

D = 8192
R = 64
ADAPTERS = 32
BLK = 128
TILE = 64
ROWS_DEV = 768
FEAT_DEV = 512
ROWS = 12288
TILES = 192
N_TENSOR = 16


def draw_tile_adapter(key, part):
    key = jax.random.fold_in(key, 11)
    order = jax.random.permutation(key, jnp.arange(TILES, dtype=jnp.int32))
    return (order % ADAPTERS).astype(jnp.int32)


def draw_tile_count(key, part):
    key = jax.random.fold_in(key, 12)
    counts = jax.random.randint(key, (TILES,), 1, TILE + 1)
    position = jnp.arange(TILES, dtype=jnp.int32)
    return jnp.where(position % (ROWS_DEV // TILE) == 0, TILE, counts).astype(jnp.int32)


def raised(result, key, source, target, parts, factor):
    owner, partner = [(jnp.arange(result.shape[dim]) // (result.shape[dim] // parts)).reshape([-1 if axis == dim else 1 for axis in range(result.ndim)]) for dim in (source, target)]
    chosen = jax.random.permutation(key, parts)[partner]
    strong = (owner == chosen) | (owner == (partner + parts // 2) % parts)
    return jnp.where(strong, factor * result, result)


def block_scale(rng, dims, shards, least, top_value):
    level, own = 1.0, jax.random.fold_in(rng, 6)
    for dim, blocks in shards:
        draws = jnp.exp(jax.random.uniform(jax.random.fold_in(own, dim), (blocks,), jnp.float32, least / len(shards), top_value / len(shards)))
        level = level * jnp.repeat(draws, dims[dim] // blocks).reshape([-1 if axis == dim else 1 for axis in range(len(dims))])
    return level


def normal_values(own_key, extent, scale, most, shards=(), held_as=jnp.bfloat16):
    values = jax.random.normal(own_key, extent, jnp.float32) * scale
    if len(shards) > 0:
        values = block_scale(own_key, extent, shards, -0.22, 0.18) * values
    return jnp.clip(values, min=-most, max=most).astype(held_as)


def noise_with(key, shape, spread, limit, split, heavy, kind=jnp.bfloat16):
    array = spread * jax.random.normal(key, shape, jnp.float32)
    if split:
        array = array * block_scale(key, shape, split, -0.22, 0.18)
    return jnp.clip(raised(array, jax.random.fold_in(key, 3), *heavy), -limit, limit).astype(kind)


def setup_inputs(seed: int = 0) -> dict:
    seeds = jax.random.split(jax.random.key(seed), 9)
    return {
        "tokens": normal_values(seeds[0], (ROWS, D), 1.0, 6.0, ((0, 16), (1, 16))),
        "base_values": noise_with(seeds[1], (D, D), D ** -0.5, 0.09375, ((0, 16),), (0, 1, 16, 2.0)),
        "base_scales": jnp.clip(jnp.exp(math.log(3.0) - 2.3025851 * jax.random.uniform(seeds[2], (D // BLK, D // BLK), jnp.float32) ** block_scale(seeds[2], (D // BLK, D // BLK), ((0, 16),), -0.2, 0.2)), 0.3, 3.0),
        "shrink_factors": normal_values(seeds[3], (ADAPTERS, D, R), D ** -0.5, 0.0625, ((0, 16), (1, 16))),
        "expand_factors": normal_values(seeds[4], (ADAPTERS, R, D), R ** -0.5, 0.75, ((0, 16), (2, 16))),
        "adapter_slot": jax.random.permutation(seeds[5], ADAPTERS).astype(jnp.int32),
        "tile_adapter": draw_tile_adapter(jax.random.fold_in(seeds[8], 71), 0),
        "tile_count": draw_tile_count(jax.random.fold_in(seeds[8], 71), 0),
    }


def reference(tokens, base_values, base_scales, shrink_factors, expand_factors, adapter_slot, tile_adapter, tile_count):
    row_count = tokens.shape[0]
    tile_total = row_count // TILE
    tile_slots = adapter_slot[tile_adapter]
    tok_tiles = tokens.reshape(tile_total, TILE, D)

    def shard_terms(shard, carry):
        base_acc, shrink_acc = carry
        first_col = (shard * FEAT_DEV).astype(jnp.int32)
        columns = lax.dynamic_slice_in_dim(tokens, first_col, FEAT_DEV, 1)
        values = lax.dynamic_slice_in_dim(base_values, first_col, FEAT_DEV, 0)
        scale_rows = lax.dynamic_slice_in_dim(base_scales, (first_col // BLK).astype(jnp.int32), FEAT_DEV // BLK, 0)
        scaled = values.reshape(FEAT_DEV // BLK, BLK, D // BLK, BLK).astype(jnp.float32) * scale_rows[:, None, :, None]
        weights = scaled.reshape(FEAT_DEV, D).astype(jnp.bfloat16)
        partial_sum = jnp.dot(columns, weights, preferred_element_type=jnp.float32)
        partial_sum = lax.optimization_barrier(partial_sum.astype(jnp.bfloat16)).astype(jnp.float32)
        factor = lax.dynamic_slice_in_dim(shrink_factors, first_col, FEAT_DEV, 1)[tile_slots]
        features = lax.dynamic_slice_in_dim(tok_tiles, first_col, FEAT_DEV, 2)
        shrink_part = jnp.einsum("tlf,tfr->tlr", features.astype(jnp.float32), factor.astype(jnp.float32))
        shrink_part = lax.optimization_barrier(shrink_part.astype(jnp.bfloat16)).astype(jnp.float32)
        return base_acc + partial_sum, shrink_acc + shrink_part

    start_carry = (jnp.zeros((row_count, D), jnp.float32), jnp.zeros((tile_total, TILE, R), jnp.float32))
    base, shrink_total = lax.fori_loop(0, N_TENSOR, shard_terms, start_carry)
    shrink = shrink_total.astype(jnp.bfloat16)
    alive = jnp.arange(TILE, dtype=jnp.int32)[None, :] < tile_count[:, None]

    def finish(item):
        shrink_tile, base_tile, slot, alive_tile = item
        delta = jnp.dot(shrink_tile, expand_factors[slot], preferred_element_type=jnp.float32)
        return (base_tile + jnp.where(alive_tile[:, None], delta, 0.0)).astype(jnp.bfloat16)

    mixed = lax.map(finish, (shrink, base.reshape(tile_total, TILE, D), tile_slots, alive))
    return mixed.reshape(row_count, D)
```

```python
import functools

import jax
import jax.numpy as jnp
from jax import lax
from jax.experimental import pallas as pl
from jax.experimental.pallas import tpu as pltpu
from jax.sharding import Mesh, PartitionSpec as P

BLK = 128
TILE = 64
AXES = ("x", "zh", "zl", "y", "c")
SIZES = (4, 4, 2, 4, 2)
VMEM_LIMIT = 56 * 1024 * 1024
F32 = jnp.float32
BF16 = jnp.bfloat16

CHUNKS = (("B", 288), ("B", 288), ("A", 192))


def shift(value, axis, step):
    size = SIZES[AXES.index(axis)]
    return lax.ppermute(value, axis, [(i, (i + step) % size) for i in range(size)])


def params(**kw):
    return pltpu.CompilerParams(vmem_limit_bytes=VMEM_LIMIT, **kw)


def cost(flops, nbytes):
    return pl.CostEstimate(flops=flops, bytes_accessed=nbytes, transcendentals=0)


def scaled(w_ref, scale_ref, block):
    rows, cols = w_ref.shape
    out = []
    for i in range(rows // BLK):
        parts = [
            (
                w_ref[i * BLK : (i + 1) * BLK, j * BLK : (j + 1) * BLK].astype(F32)
                * scale_ref[i, block * (cols // BLK) + j]
            ).astype(BF16)
            for j in range(cols // BLK)
        ]
        out.append(jnp.concatenate(parts, axis=1))
    return jnp.concatenate(out, axis=0)


def prep_kernel(blocks_ref, w_ref, scale_ref, out_ref):
    out_ref[0] = scaled(w_ref, scale_ref, blocks_ref[pl.program_id(0)])


def prep(values, scales, blocks, width):
    feats = values.shape[0]
    n = blocks.shape[0]
    return pl.pallas_call(
        prep_kernel,
        out_shape=jax.ShapeDtypeStruct((n, feats, width), BF16),
        grid_spec=pltpu.PrefetchScalarGridSpec(
            num_scalar_prefetch=1,
            grid=(n,),
            in_specs=[
                pl.BlockSpec((feats, width), lambda j, b: (0, b[j])),
                pl.BlockSpec(memory_space=pltpu.SMEM),
            ],
            out_specs=pl.BlockSpec((1, feats, width), lambda j, b: (j, 0, 0)),
        ),
        compiler_params=params(),
        cost_estimate=cost(0, 4 * n * feats * width),
        name="prep",
    )(blocks, values, scales)


def partial_kernel(plan, blocks_ref, x_ref, xs_ref, w_ref, ws_ref, scale_ref, *rest):
    outs, w_scr = rest[:-1], rest[-1]
    step = pl.program_id(0)
    w_scr[...] = scaled(w_ref, scale_ref, blocks_ref[step])
    starts = {}
    for steps, out, start, rows in plan:
        starts.setdefault((start, rows), []).append((steps, out))
    for (start, rows), stores in starts.items():
        value = (
            jnp.dot(x_ref[start : start + rows], w_scr[...], preferred_element_type=F32)
            + jnp.dot(xs_ref[start : start + rows], ws_ref[0], preferred_element_type=F32)
        ).astype(BF16)
        for steps, out in stores:
            if len(steps) == pl.num_programs(0):
                outs[out][0] = value
            else:

                @pl.when((step >= steps[0]) & (step <= steps[-1]))
                def _(out=out, value=value):
                    outs[out][0] = value


def partials(tokens, other, values, others, scales, blocks, plan):
    rows, feats = tokens.shape
    width = others.shape[2]
    n = blocks.shape[0]
    stores = [
        (tuple(range(first, first + count)), i, start, size)
        for i, (first, count, start, size) in enumerate(plan)
    ]

    def out_map(first, count):
        return lambda j, b: (jnp.clip(j - first, 0, count - 1), 0, 0)

    return pl.pallas_call(
        functools.partial(partial_kernel, stores),
        out_shape=[
            jax.ShapeDtypeStruct((count, size, width), BF16)
            for _, count, _, size in plan
        ],
        grid_spec=pltpu.PrefetchScalarGridSpec(
            num_scalar_prefetch=1,
            grid=(n,),
            in_specs=[
                pl.BlockSpec((rows, feats), lambda j, b: (0, 0)),
                pl.BlockSpec((rows, feats), lambda j, b: (0, 0)),
                pl.BlockSpec((feats, width), lambda j, b: (0, b[j])),
                pl.BlockSpec((1, feats, width), lambda j, b: (j, 0, 0)),
                pl.BlockSpec(memory_space=pltpu.SMEM),
            ],
            out_specs=[
                pl.BlockSpec((1, size, width), out_map(first, count))
                for first, count, _, size in plan
            ],
            scratch_shapes=[pltpu.VMEM((feats, width), BF16)],
        ),
        compiler_params=params(),
        cost_estimate=cost(4 * n * rows * feats * width, 2 * n * width * (2 * feats + rows)),
        name="partials",
    )(blocks, tokens, other, values, others, scales)


def whole_call(kernel, shapes, *args, name, specs=None, aliases=None):
    return pl.pallas_call(
        kernel,
        out_shape=shapes,
        in_specs=specs or [pl.BlockSpec(memory_space=pltpu.VMEM)] * len(args),
        out_specs=jax.tree.map(lambda _: pl.BlockSpec(memory_space=pltpu.VMEM), shapes),
        compiler_params=params(),
        cost_estimate=cost(0, sum(2 * a.size for a in args)),
        name=name,
    )(*args)


def plus(*parts):
    total = parts[0].astype(F32)
    for part in parts[1:]:
        total = total + part.astype(F32)
    return total.astype(BF16)


def carry_kernel(up_ref, down_ref, got_up_ref, got_down_ref, up_out, down_out):
    up_out[...] = plus(up_ref[...], got_up_ref[...])
    down_out[...] = plus(down_ref[...], got_down_ref[...])


def carry(up, down, got_up, got_down):
    count, rows, width = up.shape
    half = rows // 2
    first = pl.BlockSpec((1, half, width), lambda j: (j, 0, 0))
    second = pl.BlockSpec((1, half, width), lambda j: (j, 1, 0))
    return pl.pallas_call(
        carry_kernel,
        out_shape=[jax.ShapeDtypeStruct(up.shape, BF16)] * 2,
        grid=(count,),
        in_specs=[first, second, first, first],
        out_specs=[first, second],
        input_output_aliases={0: 0, 1: 1},
        compiler_params=params(),
        cost_estimate=cost(0, 6 * count * rows * width),
        name="carry",
    )(up, down, got_up, got_down)


def locate(slot_ref, adapter_ref, place_ref, tile):
    slot = slot_ref[adapter_ref[tile]]
    dx = lax.rem(slot // 8 - place_ref[0] + 4, 4)
    dz = lax.rem(lax.rem(slot // 2, 4) - place_ref[1] + 4, 4)
    return dx, dz * 2 + lax.rem(slot, 2)


def fetch(tiles, slot_ref, adapter_ref, place_ref, buffers, held, sems):
    own, near, far_a, far_b, back = buffers
    for t in range(tiles):
        dx, at = locate(slot_ref, adapter_ref, place_ref, t)
        for cond, ref, index in (
            (dx == 0, own, at),
            (dx == 1, near, at),
            ((dx == 2) & (at < 4), far_a, at),
            ((dx == 2) & (at >= 4), far_b, at - 4),
            (dx == 3, back, at),
        ):

            @pl.when(cond)
            def _(ref=ref, index=index, t=t):
                pltpu.make_async_copy(
                    ref.at[index], held.at[pl.ds(t * TILE, TILE)], sems.at[t]
                ).start()


def wait_for(t, buffers, held, sems):
    pltpu.make_async_copy(
        buffers[0].at[0], held.at[pl.ds(t * TILE, TILE)], sems.at[t]
    ).wait()


def shrink_kernel(slot_ref, adapter_ref, place_ref, x_ref, *rest):
    buffers, out_ref, held, sems = rest[:5], rest[5], rest[6], rest[7]
    tiles = adapter_ref.shape[0]
    fetch(tiles, slot_ref, adapter_ref, place_ref, buffers, held, sems)
    left = lax.broadcasted_iota(jnp.int32, (TILE, 2 * TILE), 1) < TILE
    for t in range(0, tiles, 2):
        wait_for(t, buffers, held, sems)
        wait_for(t + 1, buffers, held, sems)
        both = lax.dot_general(
            x_ref[t * TILE : (t + 2) * TILE],
            held[t * TILE : (t + 2) * TILE],
            (((1,), (1,)), ((), ())),
            preferred_element_type=F32,
        )
        out_ref[t * TILE // 2 : (t + 2) * TILE // 2] = jnp.where(
            left, both[:TILE], both[TILE:]
        ).astype(BF16)


def expand_kernel(slot_ref, adapter_ref, place_ref, count_ref, s0, s1, s2, s3, *rest):
    buffers, out_ref, held, sems = rest[:5], rest[5], rest[6], rest[7]
    tiles = adapter_ref.shape[0]
    fetch(tiles, slot_ref, adapter_ref, place_ref, buffers, held, sems)
    left = lax.broadcasted_iota(jnp.int32, (TILE, 2 * TILE), 1) < TILE
    for t in range(0, tiles, 2):
        wait_for(t, buffers, held, sems)
        wait_for(t + 1, buffers, held, sems)
        at = pl.ds(t * TILE // 2, TILE)
        total = (
            s0[at].astype(F32) + s1[at].astype(F32) + s2[at].astype(F32) + s3[at].astype(F32)
        )
        factors = held[t * TILE : (t + 2) * TILE]
        for k in range(2):
            shrink = jnp.where(left == (k == 0), total, 0.0).astype(BF16)
            delta = jnp.dot(shrink, factors, preferred_element_type=F32)
            row = lax.broadcasted_iota(jnp.int32, delta.shape, 0)
            out_ref[(t + k) * TILE : (t + k + 1) * TILE] = jnp.where(
                row < count_ref[t + k], delta, 0.0
            )


def with_factors(kernel, shape, scalars, arrays, buffers, width, tiles, name):
    return pl.pallas_call(
        kernel,
        out_shape=shape,
        in_specs=[pl.BlockSpec(memory_space=pltpu.SMEM)] * len(scalars)
        + [pl.BlockSpec(memory_space=pltpu.VMEM)] * len(arrays)
        + [pl.BlockSpec(memory_space=pl.ANY)] * len(buffers),
        out_specs=pl.BlockSpec(memory_space=pltpu.VMEM),
        scratch_shapes=[
            pltpu.VMEM((tiles * TILE, width), BF16),
            pltpu.SemaphoreType.DMA((tiles,)),
        ],
        compiler_params=params(),
        cost_estimate=cost(2 * tiles * TILE * TILE * width, 6 * tiles * TILE * width),
        name=name,
    )(*scalars, *arrays, *buffers)


def gather_factors(mine):
    ahead = shift(mine, "zh", -1)
    behind = shift(mine, "zh", 1)
    across = shift(mine, "zh", 2)
    line = jnp.concatenate([mine, ahead, across, behind], axis=0)
    near = shift(line, "x", -1)
    back = shift(line, "x", 1)
    far_a = shift(near[:4], "x", -1)
    far_b = shift(back[4:], "x", 1)
    return line, near, far_a, far_b, back


def finish_kernel(spans, delta_ref, *rest):
    refs, out_ref = rest[:-1], rest[-1]
    for start, rows, first, count in spans:
        total = delta_ref[start : start + rows]
        for ref in refs[first : first + count]:
            total = total + ref[0].astype(F32)
        out_ref[start : start + rows] = total.astype(BF16)


def body(
    tokens,
    base_values,
    base_scales,
    shrink_factors,
    expand_factors,
    adapter_slot,
    tile_adapter,
    tile_count,
):
    rows, feats = tokens.shape
    tiles = rows // TILE
    width = base_values.shape[1] // 16
    x, zh, zl, y, c = (lax.axis_index(name).astype(jnp.int32) for name in AXES)
    place = jnp.stack([x, zh])

    def block(core, dz, dy):
        return (zl ^ dz) * 8 + ((y + dy) % 4) * 2 + core

    order_far = [(0, 2), (1, 2)]
    order_near = [(0, 1), (1, 1), (0, 3), (1, 3), (0, 0), (1, 0)]
    far_mine = jnp.stack([block(c, *o) for o in order_far])
    near_mine = jnp.stack([block(c, *o) for o in order_near])
    far_theirs = jnp.stack([block(1 - c, *o) for o in order_far])
    near_theirs = jnp.stack([block(1 - c, *o) for o in order_near])

    other = shift(tokens, "c", 1)
    down = gather_factors(jnp.swapaxes(shrink_factors, 1, 2))
    far_weights = shift(prep(base_values, base_scales, far_theirs, width), "c", 1)
    near_weights = shift(prep(base_values, base_scales, near_theirs, width), "c", 1)
    up = gather_factors(expand_factors)

    starts, at = [], 0
    for _, size in CHUNKS:
        starts.append(at)
        at += size

    plan = []
    for (kind, size), start in zip(CHUNKS, starts):
        if kind == "B":
            half = size // 2
            plan += [(0, 2, start, half), (0, 2, start + half, half)]
        else:
            plan += [(0, 1, start, size), (1, 1, start, size)]
    far = partials(tokens, other, base_values, far_weights, base_scales, far_mine, plan)
    far = [far[2 * i : 2 * i + 2] for i in range(len(CHUNKS))]

    plan = []
    for (kind, size), start in zip(CHUNKS, starts):
        if kind == "B":
            plan += [(0, 2, start, size), (2, 2, start, size), (4, 2, start, size)]
        else:
            plan += [(j, 1, start, size) for j in range(6)]
    near = partials(tokens, other, base_values, near_weights, base_scales, near_mine, plan)

    pieces = []
    at = 0
    finals = []
    for i, ((kind, size), start) in enumerate(zip(CHUNKS, starts)):
        half = size // 2
        if kind == "B":
            up_block, down_block, own = near[at : at + 3]
            at += 3
            got_up = shift(far[i][0], "y", 1)
            got_down = shift(far[i][1], "y", -1)
            up_block, down_block = carry(up_block, down_block, got_up, got_down)
            from_below = shift(up_block, "y", 1)
            from_above = shift(down_block, "y", -1)
            leaving = plus(own[1:], from_below[1:], from_above[1:])
            got = shift(leaving, "zl", 1)
            finals.append((start, size, [own, from_below, from_above, got]))
        else:
            up0, up1, down0, down1, own0, own1 = near[at : at + 6]
            at += 6
            keep2, send2 = far[i]
            got2 = shift(send2, "zl", 1)
            got = shift(jnp.concatenate([up1, down1, own1], axis=0), "zl", 1)
            far_up = plus(keep2[:, :half], got2[:, :half])
            far_down = plus(keep2[:, half:], got2[:, half:])
            got_up = shift(far_up, "y", 1)
            got_down = shift(far_down, "y", -1)
            up_block = jnp.concatenate(
                [
                    plus(up0[:, :half], got[0:1, :half], got_up),
                    plus(up0[:, half:], got[0:1, half:]),
                ],
                axis=1,
            )
            down_block = jnp.concatenate(
                [
                    plus(down0[:, :half], got[1:2, :half]),
                    plus(down0[:, half:], got[1:2, half:], got_down),
                ],
                axis=1,
            )
            from_below = shift(up_block, "y", 1)
            from_above = shift(down_block, "y", -1)
            finals.append((start, size, [own0, got[2:], from_below, from_above]))

    scalars = (adapter_slot, tile_adapter, place)
    shrink = with_factors(
        shrink_kernel,
        jax.ShapeDtypeStruct((rows // 2, 2 * TILE), BF16),
        scalars,
        (tokens,),
        down,
        feats,
        tiles,
        "shrink",
    )
    shrink = plus(shrink, shift(shrink, "c", 1))
    shrink = plus(shrink, shift(shrink, "zl", 1))
    terms = (shrink, shift(shrink, "y", 1), shift(shrink, "y", -1), shift(shrink, "y", 2))
    delta = with_factors(
        expand_kernel,
        jax.ShapeDtypeStruct((rows, width), F32),
        scalars + (tile_count,),
        terms,
        up,
        width,
        tiles,
        "expand",
    )

    spans, args = [], []
    for start, size, parts in finals:
        spans.append((start, size, len(args), len(parts)))
        args += [(p, size) for p in parts]
    return pl.pallas_call(
        functools.partial(finish_kernel, spans),
        out_shape=jax.ShapeDtypeStruct((rows, width), BF16),
        grid=(1,),
        in_specs=[pl.BlockSpec((rows, width), lambda j: (0, 0))]
        + [pl.BlockSpec((1, size, width), lambda j: (0, 0, 0)) for _, size in args],
        out_specs=pl.BlockSpec((rows, width), lambda j: (0, 0)),
        compiler_params=params(),
        cost_estimate=cost(0, 14 * rows * width),
        name="finish",
    )(delta, *(p for p, _ in args))


def solution(mesh):
    split = Mesh(mesh.devices.reshape(SIZES), AXES)
    group, tensor = ("x", "zh"), ("zl", "y", "c")
    in_specs = (
        P(group, tensor),
        P(tensor, None),
        P(tensor, None),
        P(group, tensor, None),
        P(group, None, tensor),
        P(),
        P(group),
        P(group),
    )
    return jax.shard_map(
        body, mesh=split, in_specs=in_specs, out_specs=P(group, tensor), check_vma=False
    )
```

```python
import functools

import jax
import jax.numpy as jnp
import numpy as np
from jax import lax
from jax.experimental import pallas as pl
from jax.experimental.pallas import tpu as pltpu
from jax.sharding import Mesh, PartitionSpec as P

BLK = 128
TILE = 64
AXES = ("x", "zh", "zl", "y", "c")
SIZES = (4, 4, 2, 4, 2)
MIB = 1024 * 1024
F32 = jnp.float32
BF16 = jnp.bfloat16

CHUNKS = (384, 384)

ORDER = [(dz, e) for e in (3, 2, 1, 0) for dz in (0, 1)]
MINE, THEIRS, PLACE = 0, 8, 16


def place_table():
    rows = []
    for x, zh, zl, y, c in np.ndindex(*SIZES):
        row = []
        for core in (c, 1 - c):
            for dz, e in ORDER:
                row.append((zl ^ dz) * 8 + ((y + (1 - 2 * core) * e) % 4) * 2 + core)
        rows.append(row + [x, zh, 1 - 2 * c])
    return np.array(rows, np.int32)


def shift(value, axis, step):
    size = SIZES[AXES.index(axis)]
    return lax.ppermute(value, axis, [(i, (i + step) % size) for i in range(size)])


def turn(value, axis, step):
    size = SIZES[AXES.index(axis)]
    pairs = [
        (2 * i + core, 2 * ((i + step * (1 - 2 * core)) % size) + core)
        for i in range(size)
        for core in range(2)
    ]
    return lax.ppermute(value, (axis, "c"), pairs)


def params(mib):
    return pltpu.CompilerParams(vmem_limit_bytes=mib * MIB)


def cost(flops, nbytes):
    return pl.CostEstimate(flops=flops, bytes_accessed=nbytes, transcendentals=0)


def after(value, *deps):
    return lax.optimization_barrier((value, *deps))[0]


def scale_into(out_ref, start, w, scale_ref, block):
    rows, cols = w.shape
    for i in range(rows // BLK):
        parts = [
            (
                w[i * BLK : (i + 1) * BLK, j * BLK : (j + 1) * BLK].astype(F32)
                * scale_ref[i, block * (cols // BLK) + j]
            ).astype(BF16)
            for j in range(cols // BLK)
        ]
        out_ref[start + i * BLK : start + (i + 1) * BLK] = jnp.concatenate(parts, axis=1)


def stage_kernel(skip, meta_ref, scale_ref, w_ref, out_ref, held, done, sem_in, sem_out):
    width = held.shape[2]
    arriving, leaving = [], []
    for j in range(held.shape[0]):
        columns = pl.ds(pl.multiple_of(meta_ref[skip + j] * width, width), width)
        copy = pltpu.make_async_copy(w_ref.at[:, columns], held.at[j], sem_in.at[j])
        copy.start()
        arriving.append(copy)
    for j in range(held.shape[0]):
        arriving[j].wait()
        scale_into(done.at[j], 0, held[j], scale_ref, meta_ref[skip + j])
        copy = pltpu.make_async_copy(done.at[j], out_ref.at[j], sem_out.at[j])
        copy.start()
        leaving.append(copy)
    for copy in leaving:
        copy.wait()


def stage(values, scales, meta, skip, n, width):
    feats = values.shape[0]
    return pl.pallas_call(
        functools.partial(stage_kernel, THEIRS + skip),
        out_shape=jax.ShapeDtypeStruct((n, feats, width), BF16),
        in_specs=[
            pl.BlockSpec(memory_space=pltpu.SMEM),
            pl.BlockSpec(memory_space=pltpu.SMEM),
            pl.BlockSpec(memory_space=pl.ANY),
        ],
        out_specs=pl.BlockSpec(memory_space=pl.ANY),
        scratch_shapes=[
            pltpu.VMEM((n, feats, width), BF16),
            pltpu.VMEM((n, feats, width), BF16),
            pltpu.SemaphoreType.DMA((n,)),
            pltpu.SemaphoreType.DMA((n,)),
        ],
        compiler_params=params(16),
        cost_estimate=cost(0, 4 * n * feats * width),
        name="stage",
    )(meta, scales, values)


def partial_kernel(skip, outputs, meta_ref, x_ref, xs_ref, w_ref, ws_ref, s_ref, *rest):
    outs, scr = rest[:-1], rest[-1]
    step = pl.program_id(0)
    scale_into(scr, 0, w_ref[...], s_ref, meta_ref[skip + step])
    value = (
        jnp.dot(xs_ref[...], ws_ref[0], preferred_element_type=F32)
        + jnp.dot(x_ref[...], scr[...], preferred_element_type=F32)
    ).astype(BF16)
    for first in sorted({o[0] for o in outputs}):
        stores = [(k, o) for k, o in enumerate(outputs) if o[0] == first]

        @pl.when((step >= first) & (step < first + 2))
        def _(stores=stores):
            for k, (_, start, rows) in stores:
                outs[k][0] = value[start : start + rows]


def partials(tokens, other, values, others, scales, meta, skip, outputs):
    rows, feats = tokens.shape
    n, _, width = others.shape
    whole = pl.BlockSpec((rows, feats), lambda j, m: (0, 0))
    return pl.pallas_call(
        functools.partial(partial_kernel, MINE + skip, outputs),
        out_shape=[jax.ShapeDtypeStruct((2, size, width), BF16) for _, _, size in outputs],
        grid_spec=pltpu.PrefetchScalarGridSpec(
            num_scalar_prefetch=1,
            grid=(n,),
            in_specs=[
                whole,
                whole,
                pl.BlockSpec((feats, width), lambda j, m: (0, m[MINE + skip + j])),
                pl.BlockSpec((1, feats, width), lambda j, m: (j, 0, 0)),
                pl.BlockSpec(memory_space=pltpu.SMEM),
            ],
            out_specs=[
                pl.BlockSpec((1, size, width), lambda j, m, first=first: (jnp.clip(j - first, 0, 1), 0, 0))
                for first, _, size in outputs
            ],
            scratch_shapes=[pltpu.VMEM((feats, width), BF16)],
        ),
        compiler_params=params(30),
        cost_estimate=cost(4 * n * rows * feats * width, 2 * n * width * (2 * feats + rows)),
        name="partials",
    )(meta, tokens, other, values, others, scales)


def plus(*parts):
    total = parts[0].astype(F32)
    for part in parts[1:]:
        total = total + part.astype(F32)
    return total.astype(BF16)


def locate(slot_ref, adapter_ref, place_ref, tile):
    slot = slot_ref[adapter_ref[tile]]
    dx = (place_ref[PLACE + 2] * (lax.shift_right_logical(slot, 3) - place_ref[PLACE]) + 4) & 3
    dz = (place_ref[PLACE + 2] * ((lax.shift_right_logical(slot, 1) & 3) - place_ref[PLACE + 1]) + 4) & 3
    return dx, dz * 2 + (slot & 1)


def fetch(tiles, slot_ref, adapter_ref, place_ref, buffers, held, sems):
    for t in range(tiles):
        dx, at = locate(slot_ref, adapter_ref, place_ref, t)
        for k, ref in enumerate(buffers):

            @pl.when(dx == k)
            def _(ref=ref, at=at, t=t):
                pltpu.make_async_copy(
                    ref.at[at], held.at[pl.ds(t * TILE, TILE)], sems.at[t]
                ).start()


def wait_for(t, buffers, held, sems):
    pltpu.make_async_copy(
        buffers[0].at[0], held.at[pl.ds(t * TILE, TILE)], sems.at[t]
    ).wait()


def shrink_kernel(slot_ref, adapter_ref, place_ref, x_ref, *rest):
    buffers, out_ref, held, sems = rest[:4], rest[4], rest[5], rest[6]
    tiles = adapter_ref.shape[0]
    fetch(tiles, slot_ref, adapter_ref, place_ref, buffers, held, sems)
    left = lax.broadcasted_iota(jnp.int32, (TILE, 2 * TILE), 1) < TILE
    for t in range(0, tiles, 2):
        wait_for(t, buffers, held, sems)
        wait_for(t + 1, buffers, held, sems)
        both = lax.dot_general(
            x_ref[t * TILE : (t + 2) * TILE],
            held[t * TILE : (t + 2) * TILE],
            (((1,), (1,)), ((), ())),
            preferred_element_type=F32,
        )
        out_ref[t * TILE // 2 : (t + 2) * TILE // 2] = jnp.where(
            left, both[:TILE], both[TILE:]
        ).astype(BF16)


def expand_kernel(slot_ref, adapter_ref, place_ref, count_ref, s0, s1, s2, s3, *rest):
    buffers, out_ref, held, sems = rest[:4], rest[4], rest[5], rest[6]
    tiles = adapter_ref.shape[0]
    fetch(tiles, slot_ref, adapter_ref, place_ref, buffers, held, sems)
    left = lax.broadcasted_iota(jnp.int32, (TILE, 2 * TILE), 1) < TILE
    for t in range(0, tiles, 2):
        wait_for(t, buffers, held, sems)
        wait_for(t + 1, buffers, held, sems)
        at = pl.ds(t * TILE // 2, TILE)
        total = (
            s0[at].astype(F32) + s1[at].astype(F32) + s2[at].astype(F32) + s3[at].astype(F32)
        )
        factors = held[t * TILE : (t + 2) * TILE]
        for k in range(2):
            shrink = jnp.where(left == (k == 0), total, 0.0).astype(BF16)
            delta = jnp.dot(shrink, factors, preferred_element_type=F32)
            row = lax.broadcasted_iota(jnp.int32, delta.shape, 0)
            out_ref[(t + k) * TILE : (t + k + 1) * TILE] = jnp.where(
                row < count_ref[t + k], delta, 0.0
            )


def with_factors(kernel, shape, scalars, arrays, buffers, width, tiles, name):
    return pl.pallas_call(
        kernel,
        out_shape=shape,
        in_specs=[pl.BlockSpec(memory_space=pltpu.SMEM)] * len(scalars)
        + [pl.BlockSpec(memory_space=pltpu.VMEM)] * len(arrays)
        + [pl.BlockSpec(memory_space=pl.ANY)] * len(buffers),
        out_specs=pl.BlockSpec(memory_space=pltpu.VMEM),
        scratch_shapes=[
            pltpu.VMEM((tiles * TILE, width), BF16),
            pltpu.SemaphoreType.DMA((tiles,)),
        ],
        compiler_params=params(12),
        cost_estimate=cost(2 * tiles * TILE * TILE * width, 6 * tiles * TILE * width),
        name=name,
    )(*scalars, *arrays, *buffers)


def gather_near(mine, axis):
    return turn(mine, axis, 1), turn(mine, axis, -1)


def gather_round(mine, axis):
    behind = turn(mine, axis, 1)
    across = turn(behind, axis, 1)
    return mine, turn(across, axis, 1), across, behind


def gather_all(mine, pair, axis, *deps):
    behind, ahead = pair
    return mine, ahead, turn(after(behind, *deps), axis, 1), behind


def finish_kernel(spans, delta_ref, *rest):
    refs, out_ref = rest[:-1], rest[-1]
    for start, rows, first, count in spans:
        total = delta_ref[start : start + rows]
        for ref in refs[first : first + count]:
            total = total + ref[0].astype(F32)
        out_ref[start : start + rows] = total.astype(BF16)


def body(
    tokens,
    base_values,
    base_scales,
    shrink_factors,
    expand_factors,
    adapter_slot,
    tile_adapter,
    tile_count,
):
    rows, feats = tokens.shape
    tiles = rows // TILE
    width = base_values.shape[1] // 16
    first, second = CHUNKS
    table = jnp.asarray(place_table())
    meta = lax.dynamic_index_in_dim(table, lax.axis_index(AXES), 0, keepdims=False)

    other = shift(tokens, "c", 1)
    far_w = shift(stage(base_values, base_scales, meta, 0, 2, width), "c", 1)
    near_w = stage(base_values, base_scales, meta, 2, 6, width)

    down_mine = jnp.swapaxes(shrink_factors, 1, 2)
    behind, ahead = gather_near(down_mine, "zh")
    down_line = (down_mine, ahead, turn(down_mine, "zh", 2), behind)

    def product(weights, skip, outputs):
        return partials(tokens, other, base_values, weights, base_scales, meta, skip, outputs)

    far = product(far_w, 0, [(0, 0, first), (0, first, second)])
    near_w = shift(after(near_w, far_w, other), "c", 1)
    got1, got2 = turn(far[0], "y", 1), turn(far[1], "y", 1)

    near = product(
        after(near_w, far[0]),
        2,
        [(k, start, size) for k in (0, 2, 4) for start, size in ((0, first), (first, second))],
    )
    got1 = turn(plus(near[0], got1), "y", 1)
    got2 = turn(plus(near[1], got2), "y", 1)

    down_line = lax.optimization_barrier((*down_line, near[0]))[:4]
    down_line = jnp.concatenate(down_line, axis=0)
    down_pair = gather_near(down_line, "x")
    down = gather_all(down_line, down_pair, "x")
    up_mine = after(expand_factors, down_line)
    up_line = gather_round(up_mine, "zh")
    up_line = after(jnp.concatenate(up_line, axis=0), *down_pair)
    up = gather_all(up_line, gather_near(up_line, "x"), "x")

    got1 = turn(plus(near[2], got1), "y", 1)
    got2 = turn(plus(near[3], got2), "y", 1)

    scalars = (adapter_slot, tile_adapter, meta)
    shrink = with_factors(
        shrink_kernel,
        jax.ShapeDtypeStruct((rows // 2, 2 * TILE), BF16),
        scalars,
        (tokens,),
        down,
        feats,
        tiles,
        "shrink",
    )
    shrink = plus(shrink, shift(shrink, "c", 1))
    shrink = plus(shrink, shift(shrink, "zl", 1))
    terms = (shrink, turn(shrink, "y", 1), turn(shrink, "y", -1), turn(shrink, "y", 2))

    side1 = shift(plus(near[4][1:], got1[1:]), "zl", 1)
    side2 = shift(plus(near[5][1:], got2[1:]), "zl", 1)
    finals = [
        (0, first, [near[4], got1, side1]),
        (first, second, [near[5], got2, side2]),
    ]

    delta = with_factors(
        expand_kernel,
        jax.ShapeDtypeStruct((rows, width), F32),
        scalars + (tile_count,),
        terms,
        up,
        width,
        tiles,
        "expand",
    )

    spans, args = [], []
    for start, size, parts in finals:
        spans.append((start, size, len(args), len(parts)))
        args += [(p, size) for p in parts]
    return pl.pallas_call(
        functools.partial(finish_kernel, spans),
        out_shape=jax.ShapeDtypeStruct((rows, width), BF16),
        grid=(1,),
        in_specs=[pl.BlockSpec((rows, width), lambda j: (0, 0))]
        + [pl.BlockSpec((1, size, width), lambda j: (0, 0, 0)) for _, size in args],
        out_specs=pl.BlockSpec((rows, width), lambda j: (0, 0)),
        compiler_params=params(24),
        cost_estimate=cost(0, 14 * rows * width),
        name="finish",
    )(delta, *(p for p, _ in args))


def solution(mesh):
    split = Mesh(mesh.devices.reshape(SIZES), AXES)
    group, tensor = ("x", "zh"), ("zl", "y", "c")
    in_specs = (
        P(group, tensor),
        P(tensor, None),
        P(tensor, None),
        P(group, tensor, None),
        P(group, None, tensor),
        P(),
        P(group),
        P(group),
    )
    return jax.shard_map(
        body, mesh=split, in_specs=in_specs, out_specs=P(group, tensor), check_vma=False
    )
```

```python
import functools

import jax
import jax.numpy as jnp
import numpy as np
from jax import lax
from jax.experimental import pallas as pl
from jax.experimental.pallas import tpu as pltpu
from jax.sharding import Mesh, PartitionSpec as P

BLK = 128
TILE = 64
AXES = ("x", "zh", "zl", "y", "c")
SIZES = (4, 4, 2, 4, 2)
MIB = 1024 * 1024
F32 = jnp.float32
BF16 = jnp.bfloat16

CHUNKS = (384, 384)

ORDER = [(dz, e) for e in (3, 2, 1, 0) for dz in (0, 1)]
MINE, THEIRS, PLACE = 0, 8, 16


def place_table():
    rows = []
    for x, zh, zl, y, c in np.ndindex(*SIZES):
        row = []
        for core in (c, 1 - c):
            for dz, e in ORDER:
                row.append((zl ^ dz) * 8 + ((y + (1 - 2 * core) * e) % 4) * 2 + core)
        rows.append(row + [x, zh, 1 - 2 * c])
    return np.array(rows, np.int32)


def shift(value, axis, step):
    size = SIZES[AXES.index(axis)]
    return lax.ppermute(value, axis, [(i, (i + step) % size) for i in range(size)])


def swap(value, axis, bit):
    size = SIZES[AXES.index(axis)]
    return lax.ppermute(value, axis, [(i, i ^ bit) for i in range(size)])


def turn(value, axis, step):
    size = SIZES[AXES.index(axis)]
    pairs = [
        (2 * i + core, 2 * ((i + step * (1 - 2 * core)) % size) + core)
        for i in range(size)
        for core in range(2)
    ]
    return lax.ppermute(value, (axis, "c"), pairs)


def params(mib):
    return pltpu.CompilerParams(vmem_limit_bytes=mib * MIB)


def cost(flops, nbytes):
    return pl.CostEstimate(flops=flops, bytes_accessed=nbytes, transcendentals=0)


def after(value, *deps):
    return lax.optimization_barrier((value, *deps))[0]


def scale_into(out_ref, start, w, scale_ref, block):
    rows, cols = w.shape
    for i in range(rows // BLK):
        parts = [
            (
                w[i * BLK : (i + 1) * BLK, j * BLK : (j + 1) * BLK].astype(F32)
                * scale_ref[i, block * (cols // BLK) + j]
            ).astype(BF16)
            for j in range(cols // BLK)
        ]
        out_ref[start + i * BLK : start + (i + 1) * BLK] = jnp.concatenate(parts, axis=1)


def stage_kernel(skip, meta_ref, scale_ref, w_ref, out_ref, held, done, sem_in, sem_out):
    width = held.shape[2]
    arriving, leaving = [], []
    for j in range(held.shape[0]):
        columns = pl.ds(pl.multiple_of(meta_ref[skip + j] * width, width), width)
        copy = pltpu.make_async_copy(w_ref.at[:, columns], held.at[j], sem_in.at[j])
        copy.start()
        arriving.append(copy)
    for j in range(held.shape[0]):
        arriving[j].wait()
        scale_into(done.at[j], 0, held[j], scale_ref, meta_ref[skip + j])
        copy = pltpu.make_async_copy(done.at[j], out_ref.at[j], sem_out.at[j])
        copy.start()
        leaving.append(copy)
    for copy in leaving:
        copy.wait()


def stage(values, scales, meta, skip, n, width):
    feats = values.shape[0]
    return pl.pallas_call(
        functools.partial(stage_kernel, THEIRS + skip),
        out_shape=jax.ShapeDtypeStruct((n, feats, width), BF16),
        in_specs=[
            pl.BlockSpec(memory_space=pltpu.SMEM),
            pl.BlockSpec(memory_space=pltpu.SMEM),
            pl.BlockSpec(memory_space=pl.ANY),
        ],
        out_specs=pl.BlockSpec(memory_space=pl.ANY),
        scratch_shapes=[
            pltpu.VMEM((n, feats, width), BF16),
            pltpu.VMEM((n, feats, width), BF16),
            pltpu.SemaphoreType.DMA((n,)),
            pltpu.SemaphoreType.DMA((n,)),
        ],
        compiler_params=params(16),
        cost_estimate=cost(0, 4 * n * feats * width),
        name="stage",
    )(meta, scales, values)


def partial_kernel(skip, outputs, meta_ref, x_ref, xs_ref, w_ref, ws_ref, s_ref, *rest):
    outs, scr = rest[:-1], rest[-1]
    step = pl.program_id(0)
    scale_into(scr, 0, w_ref[...], s_ref, meta_ref[skip + step])
    value = (
        jnp.dot(xs_ref[...], ws_ref[0], preferred_element_type=F32)
        + jnp.dot(x_ref[...], scr[...], preferred_element_type=F32)
    ).astype(BF16)
    for first in sorted({o[0] for o in outputs}):
        stores = [(k, o) for k, o in enumerate(outputs) if o[0] == first]

        @pl.when((step >= first) & (step < first + 2))
        def _(stores=stores):
            for k, (_, start, rows) in stores:
                outs[k][0] = value[start : start + rows]


def partials(tokens, other, values, others, scales, meta, skip, outputs):
    rows, feats = tokens.shape
    n, _, width = others.shape
    whole = pl.BlockSpec((rows, feats), lambda j, m: (0, 0))
    return pl.pallas_call(
        functools.partial(partial_kernel, MINE + skip, outputs),
        out_shape=[jax.ShapeDtypeStruct((2, size, width), BF16) for _, _, size in outputs],
        grid_spec=pltpu.PrefetchScalarGridSpec(
            num_scalar_prefetch=1,
            grid=(n,),
            in_specs=[
                whole,
                whole,
                pl.BlockSpec((feats, width), lambda j, m: (0, m[MINE + skip + j])),
                pl.BlockSpec((1, feats, width), lambda j, m: (j, 0, 0)),
                pl.BlockSpec(memory_space=pltpu.SMEM),
            ],
            out_specs=[
                pl.BlockSpec((1, size, width), lambda j, m, first=first: (jnp.clip(j - first, 0, 1), 0, 0))
                for first, _, size in outputs
            ],
            scratch_shapes=[pltpu.VMEM((feats, width), BF16)],
        ),
        compiler_params=params(30),
        cost_estimate=cost(4 * n * rows * feats * width, 2 * n * width * (2 * feats + rows)),
        name="partials",
    )(meta, tokens, other, values, others, scales)


def plus(*parts):
    total = parts[0].astype(F32)
    for part in parts[1:]:
        total = total + part.astype(F32)
    return total.astype(BF16)


def locate(slot_ref, adapter_ref, place_ref, tile):
    slot = slot_ref[adapter_ref[tile]]
    dx = (place_ref[PLACE + 2] * (lax.shift_right_logical(slot, 3) - place_ref[PLACE]) + 4) & 3
    dz = (place_ref[PLACE + 2] * ((lax.shift_right_logical(slot, 1) & 3) - place_ref[PLACE + 1]) + 4) & 3
    return dx, dz * 2 + (slot & 1)


def fetch(tiles, slot_ref, adapter_ref, place_ref, buffers, held, sems):
    for t in range(tiles):
        dx, at = locate(slot_ref, adapter_ref, place_ref, t)
        for k, ref in enumerate(buffers):

            @pl.when(dx == k)
            def _(ref=ref, at=at, t=t):
                pltpu.make_async_copy(
                    ref.at[at], held.at[pl.ds(t * TILE, TILE)], sems.at[t]
                ).start()


def wait_for(t, buffers, held, sems):
    pltpu.make_async_copy(
        buffers[0].at[0], held.at[pl.ds(t * TILE, TILE)], sems.at[t]
    ).wait()


def shrink_kernel(slot_ref, adapter_ref, place_ref, x_ref, *rest):
    buffers, out_ref, held, sems = rest[:4], rest[4], rest[5], rest[6]
    tiles = adapter_ref.shape[0]
    fetch(tiles, slot_ref, adapter_ref, place_ref, buffers, held, sems)
    left = lax.broadcasted_iota(jnp.int32, (TILE, 2 * TILE), 1) < TILE
    for t in range(0, tiles, 2):
        wait_for(t, buffers, held, sems)
        wait_for(t + 1, buffers, held, sems)
        both = lax.dot_general(
            x_ref[t * TILE : (t + 2) * TILE],
            held[t * TILE : (t + 2) * TILE],
            (((1,), (1,)), ((), ())),
            preferred_element_type=F32,
        )
        out_ref[t * TILE // 2 : (t + 2) * TILE // 2] = jnp.where(
            left, both[:TILE], both[TILE:]
        ).astype(BF16)


def expand_kernel(slot_ref, adapter_ref, place_ref, count_ref, s0, s1, *rest):
    buffers, out_ref, held, sems = rest[:4], rest[4], rest[5], rest[6]
    tiles = adapter_ref.shape[0]
    fetch(tiles, slot_ref, adapter_ref, place_ref, buffers, held, sems)
    left = lax.broadcasted_iota(jnp.int32, (TILE, 2 * TILE), 1) < TILE
    for t in range(0, tiles, 2):
        wait_for(t, buffers, held, sems)
        wait_for(t + 1, buffers, held, sems)
        at = pl.ds(t * TILE // 2, TILE)
        total = s0[at].astype(F32) + s1[at].astype(F32)
        factors = held[t * TILE : (t + 2) * TILE]
        for k in range(2):
            shrink = jnp.where(left == (k == 0), total, 0.0).astype(BF16)
            delta = jnp.dot(shrink, factors, preferred_element_type=F32)
            row = lax.broadcasted_iota(jnp.int32, delta.shape, 0)
            out_ref[(t + k) * TILE : (t + k + 1) * TILE] = jnp.where(
                row < count_ref[t + k], delta, 0.0
            )


def with_factors(kernel, shape, scalars, arrays, buffers, width, tiles, name):
    return pl.pallas_call(
        kernel,
        out_shape=shape,
        in_specs=[pl.BlockSpec(memory_space=pltpu.SMEM)] * len(scalars)
        + [pl.BlockSpec(memory_space=pltpu.VMEM)] * len(arrays)
        + [pl.BlockSpec(memory_space=pl.ANY)] * len(buffers),
        out_specs=pl.BlockSpec(memory_space=pltpu.VMEM),
        scratch_shapes=[
            pltpu.VMEM((tiles * TILE, width), BF16),
            pltpu.SemaphoreType.DMA((tiles,)),
        ],
        compiler_params=params(12),
        cost_estimate=cost(2 * tiles * TILE * TILE * width, 6 * tiles * TILE * width),
        name=name,
    )(*scalars, *arrays, *buffers)


def gather_near(mine, axis):
    return turn(mine, axis, 1), turn(mine, axis, -1)


def gather_all(mine, pair, axis, *deps):
    behind, ahead = pair
    return mine, ahead, turn(after(behind, *deps), axis, 1), behind


def finish_kernel(spans, delta_ref, *rest):
    refs, out_ref = rest[:-1], rest[-1]
    for start, rows, first, count in spans:
        total = delta_ref[start : start + rows]
        for ref in refs[first : first + count]:
            total = total + ref[0].astype(F32)
        out_ref[start : start + rows] = total.astype(BF16)


def body(
    tokens,
    base_values,
    base_scales,
    shrink_factors,
    expand_factors,
    adapter_slot,
    tile_adapter,
    tile_count,
):
    rows, feats = tokens.shape
    tiles = rows // TILE
    width = base_values.shape[1] // 16
    first, second = CHUNKS
    table = jnp.asarray(place_table())
    meta = lax.dynamic_index_in_dim(table, lax.axis_index(AXES), 0, keepdims=False)

    other = shift(tokens, "c", 1)
    far_w = shift(stage(base_values, base_scales, meta, 0, 2, width), "c", 1)
    near_w = stage(base_values, base_scales, meta, 2, 6, width)

    down_mine = jnp.swapaxes(shrink_factors, 1, 2)
    behind, ahead = gather_near(down_mine, "zh")
    down_line = (down_mine, ahead, turn(down_mine, "zh", 2), behind)

    def product(weights, skip, outputs):
        return partials(tokens, other, base_values, weights, base_scales, meta, skip, outputs)

    far = product(far_w, 0, [(0, 0, first), (0, first, second)])
    near_w = shift(after(near_w, far_w, other), "c", 1)
    near = product(
        after(near_w, far[0]),
        2,
        [(k, start, size) for k in (0, 2, 4) for start, size in ((0, first), (first, second))],
    )

    behind = turn(after(expand_factors, far[0]), "zh", 1)
    down_line = lax.optimization_barrier((*down_line, near[0], behind))[:4]
    down_line = jnp.concatenate(down_line, axis=0)
    down_pair = gather_near(down_line, "x")
    down = gather_all(down_line, down_pair, "x")

    got1 = turn(far[0], "y", 1)
    got2 = turn(after(far[1], near[0]), "y", 1)
    got1 = turn(plus(near[0], got1), "y", 1)
    across = turn(after(behind, near[0]), "zh", 1)
    got2 = turn(plus(after(near[1], across), got2), "y", 1)
    ahead = turn(across, "zh", 1)
    got1 = turn(plus(after(near[2], ahead, *down_pair), got1), "y", 1)
    got2 = turn(plus(after(near[3], down[2]), got2), "y", 1)

    scalars = (adapter_slot, tile_adapter, meta)
    shrink = with_factors(
        shrink_kernel,
        jax.ShapeDtypeStruct((rows // 2, 2 * TILE), BF16),
        scalars,
        (tokens,),
        down,
        feats,
        tiles,
        "shrink",
    )
    up_line = jnp.concatenate([expand_factors, ahead, across, behind], axis=0)
    up_line = after(up_line, down[2])
    up = gather_all(up_line, gather_near(up_line, "x"), "x", got1)

    shrink = plus(shrink, shift(shrink, "c", 1))
    shrink = plus(shrink, shift(shrink, "zl", 1))
    shrink = plus(shrink, swap(shrink, "y", 1))
    terms = (shrink, swap(shrink, "y", 2))

    side1 = shift(plus(near[4][1:], got1[1:]), "zl", 1)
    side2 = shift(plus(near[5][1:], got2[1:]), "zl", 1)
    finals = [
        (0, first, [near[4], got1, side1]),
        (first, second, [near[5], got2, side2]),
    ]

    delta = with_factors(
        expand_kernel,
        jax.ShapeDtypeStruct((rows, width), F32),
        scalars + (tile_count,),
        terms,
        up,
        width,
        tiles,
        "expand",
    )

    spans, args = [], []
    for start, size, parts in finals:
        spans.append((start, size, len(args), len(parts)))
        args += [(p, size) for p in parts]
    return pl.pallas_call(
        functools.partial(finish_kernel, spans),
        out_shape=jax.ShapeDtypeStruct((rows, width), BF16),
        grid=(1,),
        in_specs=[pl.BlockSpec((rows, width), lambda j: (0, 0))]
        + [pl.BlockSpec((1, size, width), lambda j: (0, 0, 0)) for _, size in args],
        out_specs=pl.BlockSpec((rows, width), lambda j: (0, 0)),
        compiler_params=params(24),
        cost_estimate=cost(0, 14 * rows * width),
        name="finish",
    )(delta, *(p for p, _ in args))


def solution(mesh):
    split = Mesh(mesh.devices.reshape(SIZES), AXES)
    group, tensor = ("x", "zh"), ("zl", "y", "c")
    in_specs = (
        P(group, tensor),
        P(tensor, None),
        P(tensor, None),
        P(group, tensor, None),
        P(group, None, tensor),
        P(),
        P(group),
        P(group),
    )
    return jax.shard_map(
        body, mesh=split, in_specs=in_specs, out_specs=P(group, tensor), check_vma=False
    )
```

```python
import functools

import jax
import jax.numpy as jnp
import numpy as np
from jax import lax
from jax.experimental import pallas as pl
from jax.experimental.pallas import tpu as pltpu
from jax.sharding import Mesh, PartitionSpec as P

BLK = 128
TILE = 64
AXES = ("x", "zh", "zl", "y", "c")
SIZES = (4, 4, 2, 4, 2)
MIB = 1024 * 1024
F32 = jnp.float32
BF16 = jnp.bfloat16

CHUNKS = (416, 352)

ORDER = [(dz, e) for e in (3, 2, 1, 0) for dz in (0, 1)]
MINE, THEIRS, PLACE = 0, 8, 16


def place_table():
    rows = []
    for x, zh, zl, y, c in np.ndindex(*SIZES):
        row = []
        for core in (c, 1 - c):
            for dz, e in ORDER:
                row.append((zl ^ dz) * 8 + ((y + (1 - 2 * core) * e) % 4) * 2 + core)
        rows.append(row + [x, zh, 1 - 2 * c])
    return np.array(rows, np.int32)


def shift(value, axis, step):
    size = SIZES[AXES.index(axis)]
    return lax.ppermute(value, axis, [(i, (i + step) % size) for i in range(size)])


def swap(value, axis, bit):
    size = SIZES[AXES.index(axis)]
    return lax.ppermute(value, axis, [(i, i ^ bit) for i in range(size)])


def turn(value, axis, step):
    size = SIZES[AXES.index(axis)]
    pairs = [
        (2 * i + core, 2 * ((i + step * (1 - 2 * core)) % size) + core)
        for i in range(size)
        for core in range(2)
    ]
    return lax.ppermute(value, (axis, "c"), pairs)


def params(mib):
    return pltpu.CompilerParams(vmem_limit_bytes=mib * MIB)


def cost(flops, nbytes):
    return pl.CostEstimate(flops=flops, bytes_accessed=nbytes, transcendentals=0)


def after(value, *deps):
    return lax.optimization_barrier((value, *deps))[0]


def scale_into(out_ref, start, w, scale_ref, block):
    rows, cols = w.shape
    for i in range(rows // BLK):
        parts = [
            (
                w[i * BLK : (i + 1) * BLK, j * BLK : (j + 1) * BLK].astype(F32)
                * scale_ref[i, block * (cols // BLK) + j]
            ).astype(BF16)
            for j in range(cols // BLK)
        ]
        out_ref[start + i * BLK : start + (i + 1) * BLK] = jnp.concatenate(parts, axis=1)


def stage_kernel(skip, meta_ref, scale_ref, w_ref, out_ref, held, done, sem_in, sem_out):
    width = held.shape[2]
    arriving, leaving = [], []
    for j in range(held.shape[0]):
        columns = pl.ds(pl.multiple_of(meta_ref[skip + j] * width, width), width)
        copy = pltpu.make_async_copy(w_ref.at[:, columns], held.at[j], sem_in.at[j])
        copy.start()
        arriving.append(copy)
    for j in range(held.shape[0]):
        arriving[j].wait()
        scale_into(done.at[j], 0, held[j], scale_ref, meta_ref[skip + j])
        copy = pltpu.make_async_copy(done.at[j], out_ref.at[j], sem_out.at[j])
        copy.start()
        leaving.append(copy)
    for copy in leaving:
        copy.wait()


def stage(values, scales, meta, skip, n, width):
    feats = values.shape[0]
    return pl.pallas_call(
        functools.partial(stage_kernel, THEIRS + skip),
        out_shape=jax.ShapeDtypeStruct((n, feats, width), BF16),
        in_specs=[
            pl.BlockSpec(memory_space=pltpu.SMEM),
            pl.BlockSpec(memory_space=pltpu.SMEM),
            pl.BlockSpec(memory_space=pl.ANY),
        ],
        out_specs=pl.BlockSpec(memory_space=pl.ANY),
        scratch_shapes=[
            pltpu.VMEM((n, feats, width), BF16),
            pltpu.VMEM((n, feats, width), BF16),
            pltpu.SemaphoreType.DMA((n,)),
            pltpu.SemaphoreType.DMA((n,)),
        ],
        compiler_params=params(16),
        cost_estimate=cost(0, 4 * n * feats * width),
        name="stage",
    )(meta, scales, values)


def partial_kernel(skip, outputs, meta_ref, x_ref, xs_ref, w_ref, ws_ref, s_ref, *rest):
    outs, scr = rest[:-1], rest[-1]
    step = pl.program_id(0)
    scale_into(scr, 0, w_ref[...], s_ref, meta_ref[skip + step])
    value = (
        jnp.dot(xs_ref[...], ws_ref[0], preferred_element_type=F32)
        + jnp.dot(x_ref[...], scr[...], preferred_element_type=F32)
    ).astype(BF16)
    for first in sorted({o[0] for o in outputs}):
        stores = [(k, o) for k, o in enumerate(outputs) if o[0] == first]

        @pl.when((step >= first) & (step < first + 2))
        def _(stores=stores):
            for k, (_, start, rows) in stores:
                outs[k][0] = value[start : start + rows]


def partials(tokens, other, values, others, scales, meta, skip, outputs):
    rows, feats = tokens.shape
    n, _, width = others.shape
    whole = pl.BlockSpec((rows, feats), lambda j, m: (0, 0))
    return pl.pallas_call(
        functools.partial(partial_kernel, MINE + skip, outputs),
        out_shape=[jax.ShapeDtypeStruct((2, size, width), BF16) for _, _, size in outputs],
        grid_spec=pltpu.PrefetchScalarGridSpec(
            num_scalar_prefetch=1,
            grid=(n,),
            in_specs=[
                whole,
                whole,
                pl.BlockSpec((feats, width), lambda j, m: (0, m[MINE + skip + j])),
                pl.BlockSpec((1, feats, width), lambda j, m: (j, 0, 0)),
                pl.BlockSpec(memory_space=pltpu.SMEM),
            ],
            out_specs=[
                pl.BlockSpec((1, size, width), lambda j, m, first=first: (jnp.clip(j - first, 0, 1), 0, 0))
                for first, _, size in outputs
            ],
            scratch_shapes=[pltpu.VMEM((feats, width), BF16)],
        ),
        compiler_params=params(30),
        cost_estimate=cost(4 * n * rows * feats * width, 2 * n * width * (2 * feats + rows)),
        name="partials",
    )(meta, tokens, other, values, others, scales)


def plus(*parts):
    total = parts[0].astype(F32)
    for part in parts[1:]:
        total = total + part.astype(F32)
    return total.astype(BF16)


def locate(slot_ref, adapter_ref, place_ref, tile):
    slot = slot_ref[adapter_ref[tile]]
    dx = (place_ref[PLACE + 2] * (lax.shift_right_logical(slot, 3) - place_ref[PLACE]) + 4) & 3
    dz = (place_ref[PLACE + 2] * ((lax.shift_right_logical(slot, 1) & 3) - place_ref[PLACE + 1]) + 4) & 3
    return dx, dz * 2 + (slot & 1)


def fetch(tiles, slot_ref, adapter_ref, place_ref, buffers, held, sems):
    for t in range(tiles):
        dx, at = locate(slot_ref, adapter_ref, place_ref, t)
        for k, ref in enumerate(buffers):

            @pl.when(dx == k)
            def _(ref=ref, at=at, t=t):
                pltpu.make_async_copy(
                    ref.at[at], held.at[pl.ds(t * TILE, TILE)], sems.at[t]
                ).start()


def wait_for(t, buffers, held, sems):
    pltpu.make_async_copy(
        buffers[0].at[0], held.at[pl.ds(t * TILE, TILE)], sems.at[t]
    ).wait()


def shrink_kernel(slot_ref, adapter_ref, place_ref, x_ref, *rest):
    buffers, out_ref, held, sems = rest[:4], rest[4], rest[5], rest[6]
    tiles = adapter_ref.shape[0]
    fetch(tiles, slot_ref, adapter_ref, place_ref, buffers, held, sems)
    left = lax.broadcasted_iota(jnp.int32, (TILE, 2 * TILE), 1) < TILE
    for t in range(0, tiles, 2):
        wait_for(t, buffers, held, sems)
        wait_for(t + 1, buffers, held, sems)
        both = lax.dot_general(
            x_ref[t * TILE : (t + 2) * TILE],
            held[t * TILE : (t + 2) * TILE],
            (((1,), (1,)), ((), ())),
            preferred_element_type=F32,
        )
        out_ref[t * TILE // 2 : (t + 2) * TILE // 2] = jnp.where(
            left, both[:TILE], both[TILE:]
        ).astype(BF16)


def expand_kernel(slot_ref, adapter_ref, place_ref, count_ref, s0, s1, *rest):
    buffers, out_ref, held, sems = rest[:4], rest[4], rest[5], rest[6]
    tiles = adapter_ref.shape[0]
    fetch(tiles, slot_ref, adapter_ref, place_ref, buffers, held, sems)
    left = lax.broadcasted_iota(jnp.int32, (TILE, 2 * TILE), 1) < TILE
    for t in range(0, tiles, 2):
        wait_for(t, buffers, held, sems)
        wait_for(t + 1, buffers, held, sems)
        at = pl.ds(t * TILE // 2, TILE)
        total = s0[at].astype(F32) + s1[at].astype(F32)
        factors = held[t * TILE : (t + 2) * TILE]
        for k in range(2):
            shrink = jnp.where(left == (k == 0), total, 0.0).astype(BF16)
            delta = jnp.dot(shrink, factors, preferred_element_type=F32)
            row = lax.broadcasted_iota(jnp.int32, delta.shape, 0)
            out_ref[(t + k) * TILE : (t + k + 1) * TILE] = jnp.where(
                row < count_ref[t + k], delta, 0.0
            )


def with_factors(kernel, shape, scalars, arrays, buffers, width, tiles, name):
    return pl.pallas_call(
        kernel,
        out_shape=shape,
        in_specs=[pl.BlockSpec(memory_space=pltpu.SMEM)] * len(scalars)
        + [pl.BlockSpec(memory_space=pltpu.VMEM)] * len(arrays)
        + [pl.BlockSpec(memory_space=pl.ANY)] * len(buffers),
        out_specs=pl.BlockSpec(memory_space=pltpu.VMEM),
        scratch_shapes=[
            pltpu.VMEM((tiles * TILE, width), BF16),
            pltpu.SemaphoreType.DMA((tiles,)),
        ],
        compiler_params=params(12),
        cost_estimate=cost(2 * tiles * TILE * TILE * width, 6 * tiles * TILE * width),
        name=name,
    )(*scalars, *arrays, *buffers)


def gather_near(mine, axis):
    return turn(mine, axis, 1), turn(mine, axis, -1)


def gather_all(mine, pair, axis, *deps):
    behind, ahead = pair
    return mine, ahead, turn(after(behind, *deps), axis, 1), behind


def finish_kernel(spans, delta_ref, *rest):
    refs, out_ref = rest[:-1], rest[-1]
    for start, rows, first, count in spans:
        total = delta_ref[start : start + rows]
        for ref in refs[first : first + count]:
            total = total + ref[0].astype(F32)
        out_ref[start : start + rows] = total.astype(BF16)


def body(
    tokens,
    base_values,
    base_scales,
    shrink_factors,
    expand_factors,
    adapter_slot,
    tile_adapter,
    tile_count,
):
    rows, feats = tokens.shape
    tiles = rows // TILE
    width = base_values.shape[1] // 16
    first, second = CHUNKS
    table = jnp.asarray(place_table())
    meta = lax.dynamic_index_in_dim(table, lax.axis_index(AXES), 0, keepdims=False)

    other = shift(tokens, "c", 1)
    far_w = shift(stage(base_values, base_scales, meta, 0, 2, width), "c", 1)
    near_w = stage(base_values, base_scales, meta, 2, 6, width)

    down_mine = jnp.swapaxes(shrink_factors, 1, 2)
    def product(weights, skip, outputs):
        return partials(tokens, other, base_values, weights, base_scales, meta, skip, outputs)

    far = product(far_w, 0, [(0, 0, first), (0, first, second)])
    down_mine = after(down_mine, far[0])
    behind, ahead = gather_near(down_mine, "zh")
    down_line = (down_mine, ahead, turn(down_mine, "zh", 2), behind)
    near_w = shift(after(near_w, far_w, other), "c", 1)
    near = product(
        after(near_w, far[0]),
        2,
        [(k, start, size) for k in (0, 2, 4) for start, size in ((0, first), (first, second))],
    )

    behind = turn(after(expand_factors, far[0]), "zh", 1)
    down_line = lax.optimization_barrier((*down_line, near[0], behind))[:4]
    down_line = jnp.concatenate(down_line, axis=0)
    down_pair = gather_near(down_line, "x")

    first1 = turn(far[0], "y", 1)
    first2 = turn(far[1], "y", 1)
    mid1 = turn(plus(near[0], first1), "y", 1)
    across = turn(behind, "zh", 1)
    mid2 = turn(plus(after(near[1], across, *down_pair), first2), "y", 1)
    ahead = turn(after(across, *down_pair), "zh", 1)
    down = gather_all(down_line, down_pair, "x")
    got1 = turn(plus(near[2], mid1), "y", 1)

    scalars = (adapter_slot, tile_adapter, meta)
    shrink = with_factors(
        shrink_kernel,
        jax.ShapeDtypeStruct((rows // 2, 2 * TILE), BF16),
        scalars,
        (tokens,),
        down,
        feats,
        tiles,
        "shrink",
    )
    up_line = jnp.concatenate([expand_factors, ahead, across, behind], axis=0)
    up_line = after(up_line, shrink)
    up_pair = [turn(up_line, "x", 1), 0]
    up_pair[1] = turn(up_line, "x", -1)
    up = gather_all(up_line, up_pair, "x", got1)
    got2 = turn(plus(near[3], mid2), "y", 1)

    shrink = plus(shrink, shift(shrink, "c", 1))
    shrink = plus(shrink, shift(shrink, "zl", 1))
    zsum = shrink
    shrink = plus(shrink, swap(shrink, "y", 1))
    terms = (shrink, swap(shrink, "y", 2))
    ysum = shrink

    side1 = shift(plus(near[4][1:], got1[1:]), "zl", 1)
    side2 = shift(plus(near[5][1:], got2[1:]), "zl", 1)
    finals = [
        (0, first, [near[4], got1, side1]),
        (first, second, [near[5], got2, side2]),
    ]

    delta = with_factors(
        expand_kernel,
        jax.ShapeDtypeStruct((rows, width), F32),
        scalars + (tile_count,),
        terms,
        up,
        width,
        tiles,
        "expand",
    )

    spans, args = [], []
    for start, size, parts in finals:
        spans.append((start, size, len(args), len(parts)))
        args += [(p, size) for p in parts]
    return pl.pallas_call(
        functools.partial(finish_kernel, spans),
        out_shape=jax.ShapeDtypeStruct((rows, width), BF16),
        grid=(1,),
        in_specs=[pl.BlockSpec((rows, width), lambda j: (0, 0))]
        + [pl.BlockSpec((1, size, width), lambda j: (0, 0, 0)) for _, size in args],
        out_specs=pl.BlockSpec((rows, width), lambda j: (0, 0)),
        compiler_params=params(24),
        cost_estimate=cost(0, 14 * rows * width),
        name="finish",
    )(delta, *(p for p, _ in args))


def solution(mesh):
    split = Mesh(mesh.devices.reshape(SIZES), AXES)
    group, tensor = ("x", "zh"), ("zl", "y", "c")
    in_specs = (
        P(group, tensor),
        P(tensor, None),
        P(tensor, None),
        P(group, tensor, None),
        P(group, None, tensor),
        P(),
        P(group),
        P(group),
    )
    return jax.shard_map(
        body, mesh=split, in_specs=in_specs, out_specs=P(group, tensor), check_vma=False
    )
```

```python
import functools

import jax
import jax.numpy as jnp
import numpy as np
from jax import lax
from jax.experimental import pallas as pl
from jax.experimental.pallas import tpu as pltpu
from jax.sharding import Mesh, PartitionSpec as P

BLK = 128
TILE = 64
AXES = ("x", "zh", "zl", "y", "c")
SIZES = (4, 4, 2, 4, 2)
MIB = 1024 * 1024
F32 = jnp.float32
BF16 = jnp.bfloat16

CHUNKS = (416, 352)

ORDER = [(dz, e) for e in (3, 2, 1, 0) for dz in (0, 1)]
MINE, THEIRS, PLACE = 0, 8, 16


def place_table():
    rows = []
    for x, zh, zl, y, c in np.ndindex(*SIZES):
        row = []
        for core in (c, 1 - c):
            for dz, e in ORDER:
                row.append((zl ^ dz) * 8 + ((y + (1 - 2 * core) * e) % 4) * 2 + core)
        rows.append(row + [x, zh, 1 - 2 * c])
    return np.array(rows, np.int32)


def shift(value, axis, step):
    size = SIZES[AXES.index(axis)]
    return lax.ppermute(value, axis, [(i, (i + step) % size) for i in range(size)])


def swap(value, axis, bit):
    size = SIZES[AXES.index(axis)]
    return lax.ppermute(value, axis, [(i, i ^ bit) for i in range(size)])


def turn(value, axis, step):
    size = SIZES[AXES.index(axis)]
    pairs = [
        (2 * i + core, 2 * ((i + step * (1 - 2 * core)) % size) + core)
        for i in range(size)
        for core in range(2)
    ]
    return lax.ppermute(value, (axis, "c"), pairs)


def params(mib):
    return pltpu.CompilerParams(vmem_limit_bytes=mib * MIB)


def cost(flops, nbytes):
    return pl.CostEstimate(flops=flops, bytes_accessed=nbytes, transcendentals=0)


def after(value, *deps):
    return lax.optimization_barrier((value, *deps))[0]


def scale_into(out_ref, start, w, scale_ref, block):
    rows, cols = w.shape
    for i in range(rows // BLK):
        parts = [
            (
                w[i * BLK : (i + 1) * BLK, j * BLK : (j + 1) * BLK].astype(F32)
                * scale_ref[i, block * (cols // BLK) + j]
            ).astype(BF16)
            for j in range(cols // BLK)
        ]
        out_ref[start + i * BLK : start + (i + 1) * BLK] = jnp.concatenate(parts, axis=1)


def stage_kernel(skip, meta_ref, scale_ref, w_ref, out_ref, held, done, sem_in, sem_out):
    width = held.shape[2]
    arriving, leaving = [], []
    for j in range(held.shape[0]):
        columns = pl.ds(pl.multiple_of(meta_ref[skip + j] * width, width), width)
        copy = pltpu.make_async_copy(w_ref.at[:, columns], held.at[j], sem_in.at[j])
        copy.start()
        arriving.append(copy)
    for j in range(held.shape[0]):
        arriving[j].wait()
        scale_into(done.at[j], 0, held[j], scale_ref, meta_ref[skip + j])
        copy = pltpu.make_async_copy(done.at[j], out_ref.at[j], sem_out.at[j])
        copy.start()
        leaving.append(copy)
    for copy in leaving:
        copy.wait()


def stage(values, scales, meta, skip, n, width):
    feats = values.shape[0]
    return pl.pallas_call(
        functools.partial(stage_kernel, THEIRS + skip),
        out_shape=jax.ShapeDtypeStruct((n, feats, width), BF16),
        in_specs=[
            pl.BlockSpec(memory_space=pltpu.SMEM),
            pl.BlockSpec(memory_space=pltpu.SMEM),
            pl.BlockSpec(memory_space=pl.ANY),
        ],
        out_specs=pl.BlockSpec(memory_space=pl.ANY),
        scratch_shapes=[
            pltpu.VMEM((n, feats, width), BF16),
            pltpu.VMEM((n, feats, width), BF16),
            pltpu.SemaphoreType.DMA((n,)),
            pltpu.SemaphoreType.DMA((n,)),
        ],
        compiler_params=params(16),
        cost_estimate=cost(0, 4 * n * feats * width),
        name="stage",
    )(meta, scales, values)


def partial_kernel(skip, outputs, meta_ref, x_ref, xs_ref, w_ref, ws_ref, s_ref, *rest):
    outs, scr = rest[:-1], rest[-1]
    step = pl.program_id(0)
    scale_into(scr, 0, w_ref[...], s_ref, meta_ref[skip + step])
    value = (
        jnp.dot(xs_ref[...], ws_ref[0], preferred_element_type=F32)
        + jnp.dot(x_ref[...], scr[...], preferred_element_type=F32)
    ).astype(BF16)
    for first in sorted({o[0] for o in outputs}):
        stores = [(k, o) for k, o in enumerate(outputs) if o[0] == first]

        @pl.when((step >= first) & (step < first + 2))
        def _(stores=stores):
            for k, (_, start, rows) in stores:
                outs[k][0] = value[start : start + rows]


def partials(tokens, other, values, others, scales, meta, skip, outputs):
    rows, feats = tokens.shape
    n, _, width = others.shape
    whole = pl.BlockSpec((rows, feats), lambda j, m: (0, 0))
    return pl.pallas_call(
        functools.partial(partial_kernel, MINE + skip, outputs),
        out_shape=[jax.ShapeDtypeStruct((2, size, width), BF16) for _, _, size in outputs],
        grid_spec=pltpu.PrefetchScalarGridSpec(
            num_scalar_prefetch=1,
            grid=(n,),
            in_specs=[
                whole,
                whole,
                pl.BlockSpec((feats, width), lambda j, m: (0, m[MINE + skip + j])),
                pl.BlockSpec((1, feats, width), lambda j, m: (j, 0, 0)),
                pl.BlockSpec(memory_space=pltpu.SMEM),
            ],
            out_specs=[
                pl.BlockSpec((1, size, width), lambda j, m, first=first: (jnp.clip(j - first, 0, 1), 0, 0))
                for first, _, size in outputs
            ],
            scratch_shapes=[pltpu.VMEM((feats, width), BF16)],
        ),
        compiler_params=params(30),
        cost_estimate=cost(4 * n * rows * feats * width, 2 * n * width * (2 * feats + rows)),
        name="partials",
    )(meta, tokens, other, values, others, scales)


def plus(*parts):
    total = parts[0].astype(F32)
    for part in parts[1:]:
        total = total + part.astype(F32)
    return total.astype(BF16)


def locate(slot_ref, adapter_ref, place_ref, tile):
    slot = slot_ref[adapter_ref[tile]]
    dx = (place_ref[PLACE + 2] * (lax.shift_right_logical(slot, 3) - place_ref[PLACE]) + 4) & 3
    dz = (place_ref[PLACE + 2] * ((lax.shift_right_logical(slot, 1) & 3) - place_ref[PLACE + 1]) + 4) & 3
    return dx, dz * 2 + (slot & 1)


def fetch(tiles, slot_ref, adapter_ref, place_ref, buffers, held):
    for t in range(tiles):
        dx, at = locate(slot_ref, adapter_ref, place_ref, t)
        for k, ref in enumerate(buffers):

            @pl.when(dx == k)
            def _(ref=ref, at=at, t=t):
                held[t * TILE : (t + 1) * TILE] = ref[at]


def shrink_kernel(slot_ref, adapter_ref, place_ref, x_ref, *rest):
    buffers, out_ref, held = rest[:4], rest[4], rest[5]
    tiles = adapter_ref.shape[0]
    fetch(tiles, slot_ref, adapter_ref, place_ref, buffers, held)
    left = lax.broadcasted_iota(jnp.int32, (TILE, 2 * TILE), 1) < TILE
    for t in range(0, tiles, 2):
        both = lax.dot_general(
            x_ref[t * TILE : (t + 2) * TILE],
            held[t * TILE : (t + 2) * TILE],
            (((1,), (1,)), ((), ())),
            preferred_element_type=F32,
        )
        out_ref[t * TILE // 2 : (t + 2) * TILE // 2] = jnp.where(
            left, both[:TILE], both[TILE:]
        ).astype(BF16)


def expand_kernel(slot_ref, adapter_ref, place_ref, count_ref, s0, s1, *rest):
    buffers, out_ref, held = rest[:4], rest[4], rest[5]
    tiles = adapter_ref.shape[0]
    fetch(tiles, slot_ref, adapter_ref, place_ref, buffers, held)
    left = lax.broadcasted_iota(jnp.int32, (TILE, 2 * TILE), 1) < TILE
    for t in range(0, tiles, 2):
        at = pl.ds(t * TILE // 2, TILE)
        total = s0[at].astype(F32) + s1[at].astype(F32)
        factors = held[t * TILE : (t + 2) * TILE]
        for k in range(2):
            shrink = jnp.where(left == (k == 0), total, 0.0).astype(BF16)
            delta = jnp.dot(shrink, factors, preferred_element_type=F32)
            row = lax.broadcasted_iota(jnp.int32, delta.shape, 0)
            out_ref[(t + k) * TILE : (t + k + 1) * TILE] = jnp.where(
                row < count_ref[t + k], delta, 0.0
            )


def with_factors(kernel, shape, scalars, arrays, buffers, width, tiles, name):
    return pl.pallas_call(
        kernel,
        out_shape=shape,
        in_specs=[pl.BlockSpec(memory_space=pltpu.SMEM)] * len(scalars)
        + [pl.BlockSpec(memory_space=pltpu.VMEM)] * len(arrays)
        + [pl.BlockSpec(memory_space=pltpu.VMEM)] * len(buffers),
        out_specs=pl.BlockSpec(memory_space=pltpu.VMEM),
        scratch_shapes=[
            pltpu.VMEM((tiles * TILE, width), BF16),
        ],
        compiler_params=params(12),
        cost_estimate=cost(2 * tiles * TILE * TILE * width, 6 * tiles * TILE * width),
        name=name,
    )(*scalars, *arrays, *buffers)


def gather_near(mine, axis):
    return turn(mine, axis, 1), turn(mine, axis, -1)


def gather_all(mine, pair, axis, *deps):
    behind, ahead = pair
    return mine, ahead, turn(after(behind, *deps), axis, 1), behind


def finish_kernel(spans, delta_ref, *rest):
    refs, out_ref = rest[:-1], rest[-1]
    for start, rows, first, count in spans:
        total = delta_ref[start : start + rows]
        for ref in refs[first : first + count]:
            total = total + ref[0].astype(F32)
        out_ref[start : start + rows] = total.astype(BF16)


def body(
    tokens,
    base_values,
    base_scales,
    shrink_factors,
    expand_factors,
    adapter_slot,
    tile_adapter,
    tile_count,
):
    rows, feats = tokens.shape
    tiles = rows // TILE
    width = base_values.shape[1] // 16
    first, second = CHUNKS
    table = jnp.asarray(place_table())
    meta = lax.dynamic_index_in_dim(table, lax.axis_index(AXES), 0, keepdims=False)

    other = shift(tokens, "c", 1)
    far_w = shift(stage(base_values, base_scales, meta, 0, 2, width), "c", 1)
    near_w = stage(base_values, base_scales, meta, 2, 6, width)

    down_mine = jnp.swapaxes(shrink_factors, 1, 2)
    def product(weights, skip, outputs):
        return partials(tokens, other, base_values, weights, base_scales, meta, skip, outputs)

    far = product(far_w, 0, [(0, 0, first), (0, first, second)])
    down_mine = after(down_mine, far[0])
    behind, ahead = gather_near(down_mine, "zh")
    down_line = (down_mine, ahead, turn(down_mine, "zh", 2), behind)
    near_w = shift(after(near_w, far_w, other), "c", 1)
    near = product(
        after(near_w, far[0]),
        2,
        [(k, start, size) for k in (0, 2, 4) for start, size in ((0, first), (first, second))],
    )

    behind = turn(after(expand_factors, far[0]), "zh", 1)
    down_line = lax.optimization_barrier((*down_line, near[0], behind))[:4]
    down_line = jnp.concatenate(down_line, axis=0)
    down_pair = gather_near(down_line, "x")

    first1 = turn(far[0], "y", 1)
    first2 = turn(far[1], "y", 1)
    mid1 = turn(plus(near[0], first1), "y", 1)
    across = turn(behind, "zh", 1)
    mid2 = turn(plus(after(near[1], across, *down_pair), first2), "y", 1)
    ahead = turn(after(across, *down_pair), "zh", 1)
    down = gather_all(down_line, down_pair, "x")
    got1 = turn(plus(near[2], mid1), "y", 1)

    scalars = (adapter_slot, tile_adapter, meta)
    shrink = with_factors(
        shrink_kernel,
        jax.ShapeDtypeStruct((rows // 2, 2 * TILE), BF16),
        scalars,
        (tokens,),
        down,
        feats,
        tiles,
        "shrink",
    )
    up_line = jnp.concatenate([expand_factors, ahead, across, behind], axis=0)
    up_line = after(up_line, shrink)
    up_pair = [turn(up_line, "x", 1), 0]
    up_pair[1] = turn(up_line, "x", -1)
    up = gather_all(up_line, up_pair, "x", got1)
    got2 = turn(plus(near[3], mid2), "y", 1)

    shrink = plus(shrink, shift(shrink, "c", 1))
    shrink = plus(shrink, shift(shrink, "zl", 1))
    zsum = shrink
    shrink = plus(shrink, swap(shrink, "y", 1))
    terms = (shrink, swap(shrink, "y", 2))
    ysum = shrink

    side1 = shift(plus(near[4][1:], got1[1:]), "zl", 1)
    side2 = shift(plus(near[5][1:], got2[1:]), "zl", 1)
    finals = [
        (0, first, [near[4], got1, side1]),
        (first, second, [near[5], got2, side2]),
    ]

    delta = with_factors(
        expand_kernel,
        jax.ShapeDtypeStruct((rows, width), F32),
        scalars + (tile_count,),
        terms,
        up,
        width,
        tiles,
        "expand",
    )

    spans, args = [], []
    for start, size, parts in finals:
        spans.append((start, size, len(args), len(parts)))
        args += [(p, size) for p in parts]
    return pl.pallas_call(
        functools.partial(finish_kernel, spans),
        out_shape=jax.ShapeDtypeStruct((rows, width), BF16),
        grid=(1,),
        in_specs=[pl.BlockSpec((rows, width), lambda j: (0, 0))]
        + [pl.BlockSpec((1, size, width), lambda j: (0, 0, 0)) for _, size in args],
        out_specs=pl.BlockSpec((rows, width), lambda j: (0, 0)),
        compiler_params=params(24),
        cost_estimate=cost(0, 14 * rows * width),
        name="finish",
    )(delta, *(p for p, _ in args))


def solution(mesh):
    split = Mesh(mesh.devices.reshape(SIZES), AXES)
    group, tensor = ("x", "zh"), ("zl", "y", "c")
    in_specs = (
        P(group, tensor),
        P(tensor, None),
        P(tensor, None),
        P(group, tensor, None),
        P(group, None, tensor),
        P(),
        P(group),
        P(group),
    )
    return jax.shard_map(
        body, mesh=split, in_specs=in_specs, out_specs=P(group, tensor), check_vma=False
    )
```
